128 devices in a mesh: replica: 4 (over z_lo, core), fsdp: 32 (over y, x, z_hi).
Axes of the slice: x: 4, y: 4, z: 4 (z_hi: 2, z_lo: 2; z = z_hi * 2 + z_lo), core: 2. Of those that a mesh axis runs over, the one named last changes fastest.
Arguments:
- tokens: bfloat16 [131072, 8192], P(('replica', 'fsdp')), may hold values from -24 to 24
- out_grad: bfloat16 [131072, 512], P(('replica', 'fsdp')), may hold values from -6 to 6
- inner_weights: float32 [4, 8192, 512], P('replica', 'fsdp'), may hold values from -6 to 6
- first_moment: float32 [4, 8192, 512], P('replica', 'fsdp'), may hold values from -4 to 4
- second_moment: float32 [4, 8192, 512], P('replica', 'fsdp'), may hold values from 0.25 to 4
- global_weights: float32 [8192, 512], P('fsdp'), may hold values from -6 to 6
- outer_momentum: float32 [8192, 512], P('fsdp'), may hold values from -6 to 6
Outputs:
- new_first: float32 [4, 8192, 512], P('replica', 'fsdp')
- new_second: float32 [4, 8192, 512], P('replica', 'fsdp')
- new_global: float32 [8192, 512], P('fsdp')
- new_momentum: float32 [8192, 512], P('fsdp')
- projected: bfloat16 [131072, 512], P(('replica', 'fsdp'))
The draws below stay inside these ranges and needn't reach their ends.
All inputs are finite; a program needn't handle non-finite values.
Results may differ from the reference program's by a relative error of at most 0.0049.
Values may be sent and summed in bfloat16 or wider, within the bound.
No kernel may reach another device: no remote copies, remote signals or barrier semaphores. Data moves between devices by JAX's collectives and lax.ppermute only.
A program may use at most 128 MiB of HBM per device.

```python
import math
import jax
import jax.numpy as jnp

D = 8192
TOK_DEV = 1024
KV = 512
TOKENS = 131072
N_REPLICA = 4
N_FSDP = 32


def raised(entries, own_key, source, target, blocks, factor):
    owner, partner = [(jnp.arange(entries.shape[dim]) // (entries.shape[dim] // blocks)).reshape([-1 if axis == dim else 1 for axis in range(entries.ndim)]) for dim in (source, target)]
    chosen = jax.random.permutation(own_key, blocks)[partner]
    strong = (owner == chosen) | (owner == (partner + blocks // 2) % blocks)
    return jnp.where(strong, factor * entries, entries)


def block_scale(stream_key, dims, pieces, low, top_value):
    gain, own = 1.0, jax.random.fold_in(stream_key, 6)
    for position, blocks in pieces:
        heights = jnp.exp(jax.random.uniform(jax.random.fold_in(own, position), (blocks,), jnp.float32, low / len(pieces), top_value / len(pieces)))
        gain = gain * jnp.repeat(heights, dims[position] // blocks).reshape([-1 if axis == position else 1 for axis in range(len(dims))])
    return gain


def scatter_about(own_key, dims, spread, bound, pieces=(), dtype=jnp.bfloat16):
    result = spread * jax.random.normal(own_key, dims, jnp.float32)
    if pieces:
        result = result * block_scale(own_key, dims, pieces, -0.22, 0.18)
    return jnp.clip(result, -bound, bound).astype(dtype)


def noise_with(own_key, dims, width, reach, shards, heavy, dtype=jnp.bfloat16):
    values = width * jax.random.normal(own_key, dims, jnp.float32)
    if shards:
        values = values * block_scale(own_key, dims, shards, -0.22, 0.18)
    return jnp.clip(raised(values, jax.random.fold_in(own_key, 3), *heavy), -reach, reach).astype(dtype)


def setup_inputs(seed: int = 0) -> dict:
    keys = jax.random.split(jax.random.key(seed), 8)
    return {
        "tokens": noise_with(keys[0], (TOKENS, D), 1.0, 24.0, ((0, 128),), (0, 1, 128, 5.5)),
        "out_grad": scatter_about(keys[1], (TOKENS, KV), 1.0, 6.0, ((0, 128),)),
        "inner_weights": scatter_about(keys[2], (N_REPLICA, D, KV), 1.0, 6.0, ((0, 4), (1, 32)), jnp.float32),
        "first_moment": scatter_about(keys[3], (N_REPLICA, D, KV), 0.3, 4.0, ((0, 4), (1, 32)), jnp.float32),
        "second_moment": jnp.clip(jnp.exp(math.log(4.0) - 2.7725887 * jax.random.uniform(keys[4], (N_REPLICA, D, KV), jnp.float32) ** block_scale(keys[4], (N_REPLICA, D, KV), ((0, 4), (1, 32)), -0.2, 0.2)), 0.25, 4.0),
        "global_weights": scatter_about(keys[5], (D, KV), 1.0, 6.0, ((0, 32),), jnp.float32),
        "outer_momentum": scatter_about(keys[6], (D, KV), 0.5, 6.0, ((0, 32),), jnp.float32),
    }


def reference(tokens, out_grad, inner_weights, first_moment, second_moment, global_weights, outer_momentum):
    inv_root = 1.0 / D ** 0.5
    rows_replica = N_FSDP * TOK_DEV
    tok_all = tokens.reshape(N_REPLICA, rows_replica, D)
    grad_all = out_grad.reshape(N_REPLICA, rows_replica, KV)
    firsts = []
    seconds = []
    drift_sum = jnp.zeros((D, KV), jnp.float32)
    for replica_id in range(N_REPLICA):
        grad = jnp.dot(tok_all[replica_id].T, grad_all[replica_id], preferred_element_type=jnp.float32) * inv_root
        first = 0.9 * first_moment[replica_id] + 0.1 * grad
        second = 0.95 * second_moment[replica_id] + 0.05 * grad * grad
        inner = inner_weights[replica_id]
        stepped = inner - 0.25 * (first / (jnp.sqrt(second) + 1e-08) + 0.1 * inner)
        drift_sum = drift_sum + (global_weights - stepped)
        firsts.append(first)
        seconds.append(second)
    pseudo = drift_sum / N_REPLICA
    new_momentum = 0.9 * outer_momentum + pseudo
    new_global = global_weights - 0.7 * (pseudo + 0.9 * new_momentum)
    synced = new_global.astype(jnp.bfloat16)
    projected = (jnp.dot(tokens, synced, preferred_element_type=jnp.float32) * inv_root).astype(jnp.bfloat16)
    return (jnp.stack(firsts), jnp.stack(seconds), new_global, new_momentum, projected)
```

```python
import functools

import jax
import jax.numpy as jnp
from jax import lax
from jax.experimental import pallas as pl
from jax.experimental.pallas import tpu as pltpu
from jax.sharding import PartitionSpec as P

BOTH = ("replica", "fsdp")
BF16, F32 = jnp.bfloat16, jnp.float32
H1, H2 = (2, 1), (3, 0)


def flat(x, y, z, c):
    x, y, z = x % 4, y % 4, z % 4
    return ((z % 2) * 2 + c) * 32 + (y * 4 + x) * 2 + z // 2


def permute(array, move):
    pairs = [
        (flat(x, y, z, c), flat(*move(x, y, z, c)))
        for x in range(4)
        for y in range(4)
        for z in range(4)
        for c in range(2)
    ]
    return lax.ppermute(array, BOTH, pairs)


def along(axis, step):
    if axis == "x":
        return lambda x, y, z, c: (x + step, y, z, c)
    return lambda x, y, z, c: (x, y + step, z, c)


def other_core(x, y, z, c):
    return x, y, z, 1 - c


def pair_lo(x, y, z, c):
    return x, y, z ^ 1, c


def pair_hi(x, y, z, c):
    return x, y, 3 - z, c


def across(x, y, z, c):
    return x, y, z + 2, c


AXES = (("x", "y"), ("y", "x"))


def place():
    f = lax.axis_index("fsdp")
    return f // 8, (f // 2) % 4, f % 2


def numbers(blocks):
    y, x, _ = place()
    found = []
    for kind, k1, k2 in blocks:
        dx, dy = (k1, k2) if kind == 0 else (k2, k1)
        found.append((((y + dy) % 4) * 4 + (x + dx) % 4) * 2 + kind)
    return jnp.stack(found).astype(jnp.int32)


def grad_kernel(groups, size, n_recv, idx_ref, tok_ref, g_ref, *refs):
    recv, outs = refs[:n_recv], refs[n_recv:]
    step = pl.program_id(0)
    term = lax.dot_general(
        tok_ref[...], g_ref[...], (((0,), (0,)), ((), ())), preferred_element_type=F32
    )
    for group in range(groups):

        @pl.when(step // size == group)
        def _(group=group):
            total = term
            if n_recv:
                total = total + recv[group][0].astype(F32)
            outs[group][0] = total.astype(outs[group].dtype)


def grad_blocks(blocks, groups, tokens, out_grad, recv=(), dtype=BF16):
    size = len(blocks) // groups
    rows = tokens.shape[1] // 32
    cols = out_grad.shape[1]
    toks = tokens.shape[0]

    def part(group):
        return pl.BlockSpec(
            (1, rows, cols), lambda i, idx: (jnp.clip(i - group * size, 0, size - 1), 0, 0)
        )

    return pl.pallas_call(
        functools.partial(grad_kernel, groups, size, len(recv)),
        grid_spec=pltpu.PrefetchScalarGridSpec(
            num_scalar_prefetch=1,
            grid=(len(blocks),),
            in_specs=[
                pl.BlockSpec((toks, rows), lambda i, idx: (0, idx[i])),
                pl.BlockSpec((toks, cols), lambda i, idx: (0, 0)),
                *[part(group) for group in range(len(recv))],
            ],
            out_specs=[part(group) for group in range(groups)],
        ),
        out_shape=[jax.ShapeDtypeStruct((size, rows, cols), dtype) for _ in range(groups)],
        compiler_params=pltpu.CompilerParams(vmem_limit_bytes=50 << 20),
        cost_estimate=pl.CostEstimate(
            flops=2 * toks * rows * cols * len(blocks),
            bytes_accessed=2 * toks * rows * len(blocks),
            transcendentals=0,
        ),
    )(numbers(blocks), tokens, out_grad, *recv)


def project_kernel(sizes, has_acc, last, scale, idx_ref, core_ref, tok_ref, *refs):
    n = len(sizes)
    mine, theirs = refs[:n], refs[n : 2 * n]
    refs = refs[2 * n :]
    if has_acc:
        acc_in, refs = refs[0], refs[1:]
    out_ref = refs[0]
    acc = refs[1] if last else out_ref
    step = pl.program_id(0)

    @pl.when(step == 0)
    def _():
        if has_acc:
            acc[...] = acc_in[...]
        else:
            acc[...] = jnp.zeros_like(acc)

    start = 0
    for group, size in enumerate(sizes):

        @pl.when((step >= start) & (step < start + size))
        def _(group=group):
            acc[0] += jnp.dot(tok_ref[...], mine[group][0], preferred_element_type=F32)
            acc[1] += jnp.dot(tok_ref[...], theirs[group][0], preferred_element_type=F32)

        start += size
    if last:
        half = acc.shape[2]
        for core in range(2):

            @pl.when((step == start - 1) & (core_ref[0] == core))
            def _(core=core):
                out_ref[:, core * half : (core + 1) * half] = (acc[0] * scale).astype(BF16)
                out_ref[:, (1 - core) * half : (2 - core) * half] = (acc[1] * scale).astype(BF16)


def project_blocks(blocks, mine, theirs, acc, last, tokens, core, scale):
    sizes = [array.shape[0] for array in mine]
    toks = tokens.shape[0]
    rows, half = mine[0].shape[1:]

    def part(group):
        start, size = sum(sizes[:group]), sizes[group]
        return pl.BlockSpec(
            (1, rows, half), lambda i, idx, core: (jnp.clip(i - start, 0, size - 1), 0, 0)
        )

    parts = [part(group) for group in range(len(sizes))]
    whole = pl.BlockSpec((2, toks, half), lambda i, idx, core: (0, 0, 0))
    if last:
        out_shape = jax.ShapeDtypeStruct((toks, 2 * half), BF16)
        out_spec = pl.BlockSpec((toks, 2 * half), lambda i, idx, core: (0, 0))
    else:
        out_shape = jax.ShapeDtypeStruct((2, toks, half), F32)
        out_spec = whole
    carried = [] if acc is None else [acc]
    return pl.pallas_call(
        functools.partial(project_kernel, sizes, bool(carried), last, scale),
        grid_spec=pltpu.PrefetchScalarGridSpec(
            num_scalar_prefetch=2,
            grid=(sum(sizes),),
            in_specs=[
                pl.BlockSpec((toks, rows), lambda i, idx, core: (0, idx[i])),
                *parts,
                *parts,
                *[whole for _ in carried],
            ],
            out_specs=out_spec,
            scratch_shapes=[pltpu.VMEM((2, toks, half), F32)] if last else [],
        ),
        out_shape=out_shape,
        compiler_params=pltpu.CompilerParams(vmem_limit_bytes=50 << 20),
        cost_estimate=pl.CostEstimate(
            flops=4 * toks * rows * half * sum(sizes),
            bytes_accessed=2 * toks * rows * sum(sizes),
            transcendentals=0,
        ),
    )(numbers(blocks), core[None], tokens, *mine, *theirs, *carried)


def pick(k1, half):
    return [[(kind, k1, k2) for k2 in half] for kind in range(2)]


def reduce_scatter(tokens, out_grad):
    kinds = range(2)
    blocks = functools.partial(grad_blocks, tokens=tokens, out_grad=out_grad)

    def lay(forward, backward):
        order = []
        for kind in kinds:
            for k1, half in (forward, backward):
                order += [(kind, k1, k2) for k2 in half]
        return order

    def send(four):
        got = []
        for kind in kinds:
            axis = AXES[kind][0]
            got.append(permute(four[2 * kind], along(axis, 1)))
            got.append(permute(four[2 * kind + 1], along(axis, -1)))
        return got

    first = send(blocks(lay((2, H1), (2, H2)), 4))
    second = send(blocks(lay((1, H2), (3, H1)), 4))
    third = send(blocks(lay((1, H1), (3, H2)), 4, recv=first))
    own = blocks([(kind, 0, k2) for kind in kinds for k2 in H1 + H2], 2, dtype=F32)
    finals = []
    for kind in kinds:
        axis = AXES[kind][1]
        up2, down2 = second[2 * kind : 2 * kind + 2]
        up3, down3 = third[2 * kind : 2 * kind + 2]
        sums = {}
        for place_in, k2 in enumerate(H1):
            sums[k2] = (
                own[kind][place_in] + up3[place_in].astype(F32) + down2[place_in].astype(F32)
            )
        for place_in, k2 in enumerate(H2):
            sums[k2] = (
                own[kind][2 + place_in] + up2[place_in].astype(F32) + down3[place_in].astype(F32)
            )
        cut = sums[2].shape[0] // 2
        far = sums[2].astype(BF16)
        up = permute(far[:cut], along(axis, 1)).astype(F32)
        down = permute(far[cut:], along(axis, -1)).astype(F32)
        near = jnp.concatenate([sums[1][:cut] + up, sums[1][cut:]]).astype(BF16)
        back = jnp.concatenate([sums[3][:cut], sums[3][cut:] + down]).astype(BF16)
        finals.append(
            sums[0]
            + permute(near, along(axis, 1)).astype(F32)
            + permute(back, along(axis, -1)).astype(F32)
        )
    even = place()[2] == 0
    keep = jnp.where(even, finals[0], finals[1])
    give = jnp.where(even, finals[1], finals[0]).astype(BF16)
    return keep + permute(give, across).astype(F32)


def ring_gather(block, axis):
    behind = permute(block, along(axis, 1))
    ahead = permute(block, along(axis, -1))
    return behind, ahead


def gather_project(synced, tokens, core, scale):
    received = permute(synced, pair_hi)
    even = place()[2] == 0
    own = [jnp.where(even, synced, received), jnp.where(even, received, synced)]
    cut = synced.shape[0] // 2
    stacks = []
    for kind in range(2):
        axis = AXES[kind][0]
        behind, ahead = ring_gather(own[kind], axis)
        low = permute(behind[:cut], along(axis, 1))
        high = permute(ahead[cut:], along(axis, -1))
        stacks.append(jnp.stack([own[kind], behind, ahead, jnp.concatenate([low, high])]))
    order = (0, 3, 1, 2)

    def swap(arrays):
        return [permute(array, other_core) for array in arrays]

    run = functools.partial(project_blocks, tokens=tokens, core=core, scale=scale)
    acc = run(
        [(kind, k1, 0) for kind in range(2) for k1 in order], stacks, swap(stacks), None, False
    )
    behinds, aheads, near = [], [], []
    for kind in range(2):
        behind, ahead = ring_gather(stacks[kind], AXES[kind][1])
        behinds.append(behind)
        aheads.append(ahead)
        near += [behind, ahead]
    acc = run(
        [(kind, k1, k2) for kind in range(2) for k2 in (3, 1) for k1 in order],
        near,
        swap(near),
        acc,
        False,
    )
    far = []
    for kind in range(2):
        axis = AXES[kind][1]
        far.append(permute(behinds[kind][:2], along(axis, 1)))
        far.append(permute(aheads[kind][2:], along(axis, -1)))
    return run(
        [(kind, k1, 2) for kind in range(2) for k1 in order], far, swap(far), acc, True
    )


def body(
    tokens, out_grad, inner_weights, first_moment, second_moment, global_weights, outer_momentum
):
    scale = 1.0 / tokens.shape[1] ** 0.5
    core = (lax.axis_index("replica") % 2).astype(jnp.int32)
    grad = reduce_scatter(tokens, out_grad) * scale
    first = 0.9 * first_moment[0] + 0.1 * grad
    second = 0.95 * second_moment[0] + 0.05 * grad * grad
    inner = inner_weights[0]
    stepped = inner - 0.25 * (first / (jnp.sqrt(second) + 1e-08) + 0.1 * inner)
    drift = global_weights - stepped
    n_replica = lax.axis_size("replica")
    half = drift.shape[1] // 2

    def outer(total, weights, momentum):
        pseudo = total / n_replica
        new_momentum = 0.9 * momentum + pseudo
        return weights - 0.7 * (pseudo + 0.9 * new_momentum), new_momentum

    def columns(array, which):
        return lax.dynamic_slice_in_dim(array, which * half, half, axis=1)

    mine = columns(drift, core) + permute(columns(drift, 1 - core), other_core)
    mine = mine + permute(mine, pair_lo)
    synced = outer(mine, columns(global_weights, core), columns(outer_momentum, core))[0]
    theirs = permute(mine, other_core)
    total = jnp.where(
        core == 0,
        jnp.concatenate([mine, theirs], axis=1),
        jnp.concatenate([theirs, mine], axis=1),
    )
    new_global, new_momentum = outer(total, global_weights, outer_momentum)
    projected = gather_project(synced.astype(BF16), tokens, core, scale)
    return (first[None], second[None], new_global, new_momentum, projected)


def solution(mesh):
    placed = (
        P(("replica", "fsdp"), None),
        P(("replica", "fsdp"), None),
        P("replica", "fsdp", None),
        P("replica", "fsdp", None),
        P("replica", "fsdp", None),
        P("fsdp", None),
        P("fsdp", None),
    )
    return jax.shard_map(
        body,
        mesh=mesh,
        in_specs=placed,
        out_specs=(
            P("replica", "fsdp", None),
            P("replica", "fsdp", None),
            P("fsdp", None),
            P("fsdp", None),
            P(("replica", "fsdp"), None),
        ),
        check_vma=False,
    )
```

```python
import functools

import jax
import jax.numpy as jnp
from jax import lax
from jax.experimental import pallas as pl
from jax.experimental.pallas import tpu as pltpu
from jax.sharding import PartitionSpec as P

BOTH = ("replica", "fsdp")
BF16, F32 = jnp.bfloat16, jnp.float32
H1, H2 = (2, 1), (3, 0)
VMEM = pl.BlockSpec(memory_space=pltpu.VMEM)
ANY = pl.BlockSpec(memory_space=pl.ANY)


def flat(x, y, z, c):
    x, y, z = x % 4, y % 4, z % 4
    return ((z % 2) * 2 + c) * 32 + (y * 4 + x) * 2 + z // 2


def permute(array, move):
    pairs = []
    for x in range(4):
        for y in range(4):
            for z in range(4):
                for c in range(2):
                    target = move(x, y, z, c)
                    if target is not None:
                        pairs.append((flat(x, y, z, c), flat(*target)))
    return lax.ppermute(array, BOTH, pairs)


def first(step):
    return lambda x, y, z, c: (x, y + step, z, c) if c else (x + step, y, z, c)


def second(step):
    return lambda x, y, z, c: (x + step, y, z, c) if c else (x, y + step, z, c)


def other_core(x, y, z, c):
    return x, y, z, 1 - c


def pair_lo(x, y, z, c):
    return x, y, z ^ 1, c


def pair_hi(x, y, z, c):
    return None if z // 2 == c else (x, y, 3 - z, 1 - c)


def across(x, y, z, c):
    return x, y, z + 2, c


def z_hi():
    return lax.rem(lax.axis_index("fsdp"), 2)


def core_index():
    return lax.rem(lax.axis_index("replica"), 2)


def plane(core, k1, k2):
    f = lax.axis_index("fsdp")
    y, x = lax.div(f, 8), lax.rem(lax.div(f, 2), 4)
    dx, dy = k1 + core * (k2 - k1), k2 + core * (k1 - k2)
    return lax.rem(y + dy, 4) * 4 + lax.rem(x + dx, 4)


def local(kernel, outs, *arrays, limit=16):
    return pl.pallas_call(
        kernel,
        in_specs=[VMEM] * len(arrays),
        out_specs=[VMEM] * len(outs),
        out_shape=[jax.ShapeDtypeStruct(*out) for out in outs],
        compiler_params=pltpu.CompilerParams(vmem_limit_bytes=limit << 20),
    )(*arrays)


def columns(tok_ref, start, width):
    return tok_ref.at[:, pl.ds(pl.multiple_of(start, 256), width)]


def started(copies):
    for copy in copies:
        copy.start()
    return copies


def cost(rows, width, cols):
    return pl.CostEstimate(
        flops=2 * rows * width * cols, bytes_accessed=2 * rows * width, transcendentals=0
    )


def grad_kernel(names, n_recv, tok_ref, grad_ref, *refs):
    groups = len(names) // 2
    recv, outs = refs[:n_recv], refs[n_recv : n_recv + groups]
    held, g_ref, sems = refs[n_recv + groups :]
    g_copy = pltpu.make_async_copy(grad_ref, g_ref, sems.at[len(names)])
    g_copy.start()
    copies = started(
        [
            pltpu.make_async_copy(
                columns(tok_ref, plane(core_index(), *name) * 512, 512),
                held.at[:, 512 * number : 512 * number + 512],
                sems.at[number],
            )
            for number, name in enumerate(names)
        ]
    )
    g_copy.wait()
    for number in range(len(names)):
        copies[number].wait()
        group, rows = number // 2, slice(512 * (number % 2), 512 * (number % 2) + 512)
        term = lax.dot_general(
            held[:, 512 * number : 512 * number + 512],
            g_ref[...],
            (((0,), (0,)), ((), ())),
            preferred_element_type=F32,
        )
        if recv:
            term = term + recv[group][rows].astype(F32)
        outs[group][rows] = term.astype(outs[group].dtype)


def grad_blocks(groups, dtype, limit, tokens, out_grad, *recv):
    names = [(k1, k2) for k1, half in groups for k2 in half]
    width, cols = 512 * len(names), out_grad.shape[1]
    return pl.pallas_call(
        functools.partial(grad_kernel, names, len(recv)),
        in_specs=[ANY, ANY] + [VMEM] * len(recv),
        out_specs=[VMEM] * len(groups),
        out_shape=[jax.ShapeDtypeStruct((1024, cols), dtype)] * len(groups),
        scratch_shapes=[
            pltpu.VMEM((tokens.shape[0], width), BF16),
            pltpu.VMEM(out_grad.shape, BF16),
            pltpu.SemaphoreType.DMA((len(names) + 1,)),
        ],
        compiler_params=pltpu.CompilerParams(vmem_limit_bytes=limit << 20),
        cost_estimate=cost(tokens.shape[0], width, cols),
    )(tokens, out_grad, *recv)


def total_kernel(own1, own2, got1, got2, two, one, three, zero):
    for out, own, got, rows in (
        (two, own1, got1, slice(0, 512)),
        (one, own1, got1, slice(512, 1024)),
        (three, own2, got2, slice(0, 512)),
        (zero, own2, got2, slice(512, 1024)),
    ):
        out[...] = (own[rows] + got[rows].astype(F32)).astype(out.dtype)


def choose_kernel(zero, two, one, three, keep, give):
    rows = keep.shape[0]
    mine = z_hi()
    for which, out in ((mine, keep), (1 - mine, give)):
        part = pl.ds(pl.multiple_of(which * rows, rows), rows)
        total = zero[part]
        for ref in (two, one, three):
            total = total + ref[part].astype(F32)
        out[...] = total.astype(out.dtype)


def reduce_scatter(tokens, out_grad):
    def send(arrays):
        return permute(arrays[0], first(1)), permute(arrays[1], first(-1))

    def blocks(groups, dtype, limit, *recv):
        return grad_blocks(groups, dtype, limit, tokens, out_grad, *recv)

    up1, down1 = send(blocks([(2, H1), (2, H2)], BF16, 50))
    up2, down2 = send(blocks([(1, H2), (3, H1)], BF16, 46))
    up3, down3 = send(blocks([(1, H1), (3, H2)], BF16, 46, up1, down1))
    own1, own2 = blocks([(0, H1), (0, H2)], F32, 46, down2, up2)
    block = (512, 512)
    two, one, three, zero = local(
        total_kernel,
        [(block, BF16), (block, BF16), (block, BF16), (block, F32)],
        own1,
        own2,
        up3,
        down3,
    )
    keep, give = local(
        choose_kernel,
        [((256, 512), F32), ((256, 512), BF16)],
        zero,
        permute(two, second(2)),
        permute(one, second(1)),
        permute(three, second(-1)),
    )
    return keep, permute(give, across)


def update_kernel(
    scale, keep, got, inner_ref, first_ref, second_ref, weights_ref, first_out, second_out, mine, other
):
    grad = (keep[...] + got[...].astype(F32)) * scale
    new_first = 0.9 * first_ref[...] + 0.1 * grad
    new_second = 0.95 * second_ref[...] + 0.05 * grad * grad
    inner = inner_ref[...]
    stepped = inner - 0.25 * (new_first / (jnp.sqrt(new_second) + 1e-08) + 0.1 * inner)
    drift = weights_ref[...] - stepped
    first_out[...] = new_first
    second_out[...] = new_second
    half = drift.shape[1] // 2
    core = core_index()
    for which, out in ((core, mine), (1 - core, other)):
        out[...] = jnp.where(which == 0, drift[:, :half], drift[:, half:])


def add_kernel(left, right, out):
    out[...] = left[...] + right[...]


def outer_kernel(
    n_replica, mine, theirs, weights_ref, momentum_ref, weights_out, momentum_out, synced
):
    half = mine.shape[1]
    low = core_index() == 0
    left, right = mine[...], theirs[...]
    for part, total in (
        (slice(0, half), jnp.where(low, left, right)),
        (slice(half, 2 * half), jnp.where(low, right, left)),
    ):
        pseudo = total / n_replica
        new_momentum = 0.9 * momentum_ref[:, part] + pseudo
        new_global = weights_ref[:, part] - 0.7 * (pseudo + 0.9 * new_momentum)
        weights_out[:, part] = new_global
        momentum_out[:, part] = new_momentum
        synced[:, part] = new_global.astype(BF16)


def pick_kernel(synced, got, out):
    out[...] = jnp.where(z_hi() == core_index(), synced[...], got[...])


def stack_kernel(*refs):
    ins, outs = refs[:4], refs[4:]
    for number, ref in enumerate(ins):
        at = 256 * (number % 2)
        outs[number // 2][at : at + 256] = ref[...]


def project_kernel(places, n_recv, carried, scale, tok_ref, *refs):
    arrays = refs[:n_recv]
    acc = refs[n_recv] if carried else None
    out, held, right, sems = refs[-4:]
    copies, at = [], 0
    for number, (ref, (partner, names)) in enumerate(zip(arrays, places)):
        core = core_index()
        who = 1 - core if partner else core
        batch = [
            pltpu.make_async_copy(
                columns(tok_ref, plane(who, *name) * 512 + who * 256, 256),
                held.at[:, at + 256 * place : at + 256 * place + 256],
                sems.at[3 * number + place],
            )
            for place, name in enumerate(names)
        ]
        batch.append(
            pltpu.make_async_copy(ref, right.at[at : at + 512], sems.at[3 * number + 2])
        )
        copies += started(batch)
        at += 512
    total = acc[...] if carried else None
    step = 1024
    for start in range(0, at, step):
        for copy in copies[3 * start // 512 : 3 * (start + step) // 512]:
            copy.wait()
        term = jnp.dot(
            held[:, start : start + step],
            right[start : start + step],
            preferred_element_type=F32,
        )
        total = term if total is None else total + term
    out[...] = total if scale is None else (total * scale).astype(BF16)


def project(tokens, arrays, names, acc, scale):
    theirs = [permute(array, other_core) for array in arrays]
    both = [*arrays, *theirs]
    places = [(0, name) for name in names] + [(1, name) for name in names]
    carried = [] if acc is None else [acc]
    rows, width, cols = tokens.shape[0], 512 * len(both), arrays[0].shape[1]
    return pl.pallas_call(
        functools.partial(project_kernel, places, len(both), bool(carried), scale),
        in_specs=[ANY] + [ANY] * len(both) + [VMEM] * len(carried),
        out_specs=VMEM,
        out_shape=jax.ShapeDtypeStruct((rows, cols), F32 if scale is None else BF16),
        scratch_shapes=[
            pltpu.VMEM((rows, width), BF16),
            pltpu.VMEM((width, cols), BF16),
            pltpu.SemaphoreType.DMA((3 * len(both),)),
        ],
        compiler_params=pltpu.CompilerParams(vmem_limit_bytes=46 << 20),
        cost_estimate=cost(rows, width, cols),
    )(tokens, *both, *carried)


def gather_project(synced, tokens, scale):
    quarter = ((256, 512), BF16)
    half = ((512, 512), BF16)
    (own,) = local(pick_kernel, [quarter], synced, permute(synced, pair_hi))
    far = permute(own, first(2))
    behind, ahead = permute(own, first(1)), permute(own, first(-1))
    low, high = local(stack_kernel, [half, half], own, behind, ahead, far)
    lows, highs = (0, 3), (1, 2)
    low_up, high_down = permute(low, second(1)), permute(high, second(-1))
    high_up, low_down = permute(high, second(1)), permute(low, second(-1))
    low_far, high_far = permute(low_up, second(1)), permute(high_down, second(-1))

    def names(firsts, k2):
        return [(k1, k2) for k1 in firsts]

    acc = project(tokens, [low, high], [names(lows, 0), names(highs, 0)], None, None)
    acc = project(tokens, [low_up, high_down], [names(lows, 3), names(highs, 1)], acc, None)
    acc = project(tokens, [high_up, low_down], [names(highs, 3), names(lows, 1)], acc, None)
    return project(tokens, [low_far, high_far], [names(lows, 2), names(highs, 2)], acc, scale)


def body(
    tokens, out_grad, inner_weights, first_moment, second_moment, global_weights, outer_momentum
):
    scale = 1.0 / tokens.shape[1] ** 0.5
    n_replica = lax.axis_size("replica")
    keep, got = reduce_scatter(tokens, out_grad)
    block, half = keep.shape, (keep.shape[0], keep.shape[1] // 2)
    new_first, new_second, mine, other = local(
        functools.partial(update_kernel, scale),
        [(block, F32), (block, F32), (half, F32), (half, F32)],
        keep,
        got,
        inner_weights[0],
        first_moment[0],
        second_moment[0],
        global_weights,
    )
    (mine,) = local(add_kernel, [(half, F32)], mine, permute(other, other_core))
    (mine,) = local(add_kernel, [(half, F32)], mine, permute(mine, pair_lo))
    new_global, new_momentum, synced = local(
        functools.partial(outer_kernel, n_replica),
        [(block, F32), (block, F32), (block, BF16)],
        mine,
        permute(mine, other_core),
        global_weights,
        outer_momentum,
    )
    projected = gather_project(synced, tokens, scale)
    return (new_first[None], new_second[None], new_global, new_momentum, projected)


def solution(mesh):
    placed = (
        P(("replica", "fsdp"), None),
        P(("replica", "fsdp"), None),
        P("replica", "fsdp", None),
        P("replica", "fsdp", None),
        P("replica", "fsdp", None),
        P("fsdp", None),
        P("fsdp", None),
    )
    return jax.shard_map(
        body,
        mesh=mesh,
        in_specs=placed,
        out_specs=(
            P("replica", "fsdp", None),
            P("replica", "fsdp", None),
            P("fsdp", None),
            P("fsdp", None),
            P(("replica", "fsdp"), None),
        ),
        check_vma=False,
    )
```

```python
import functools

import jax
import jax.numpy as jnp
from jax import lax
from jax.experimental import pallas as pl
from jax.experimental.pallas import tpu as pltpu
from jax.sharding import PartitionSpec as P

BOTH = ("replica", "fsdp")
BF16, F32 = jnp.bfloat16, jnp.float32
H1, H2 = (2, 1), (3, 0)
VMEM = pl.BlockSpec(memory_space=pltpu.VMEM)
ANY = pl.BlockSpec(memory_space=pl.ANY)
SMALL = pl.CostEstimate(flops=1, bytes_accessed=1, transcendentals=0)


def flat(x, y, z, c):
    x, y, z = x % 4, y % 4, z % 4
    return ((z % 2) * 2 + c) * 32 + (y * 4 + x) * 2 + z // 2


def permute(array, move):
    pairs = []
    for x in range(4):
        for y in range(4):
            for z in range(4):
                for c in range(2):
                    target = move(x, y, z, c)
                    if target is not None:
                        pairs.append((flat(x, y, z, c), flat(*target)))
    return lax.ppermute(array, BOTH, pairs)


def first(step):
    return lambda x, y, z, c: (x, y + step, z, c) if c else (x + step, y, z, c)


def second(step):
    return lambda x, y, z, c: (x + step, y, z, c) if c else (x, y + step, z, c)


def other_core(x, y, z, c):
    return x, y, z, 1 - c


def pair_lo(x, y, z, c):
    return x, y, z ^ 1, c


def halves_one(x, y, z, c):
    return (x, y, 3 - z, c) if z // 2 == c else (x, y, z, 1 - c)


def halves_two(x, y, z, c):
    return None if z // 2 == c else (x, y, 3 - z, 1 - c)


def across(x, y, z, c):
    return x, y, z + 2, c


def z_hi():
    return lax.rem(lax.axis_index("fsdp"), 2)


def core_index():
    return lax.rem(lax.axis_index("replica"), 2)


def plane(core, k1, k2):
    f = lax.axis_index("fsdp")
    y, x = lax.div(f, 8), lax.rem(lax.div(f, 2), 4)
    dx, dy = k1 + core * (k2 - k1), k2 + core * (k1 - k2)
    return lax.rem(y + dy, 4) * 4 + lax.rem(x + dx, 4)


def local(kernel, outs, *arrays, limit=16):
    return pl.pallas_call(
        kernel,
        in_specs=[VMEM] * len(arrays),
        out_specs=[VMEM] * len(outs),
        out_shape=[jax.ShapeDtypeStruct(*out) for out in outs],
        compiler_params=pltpu.CompilerParams(vmem_limit_bytes=limit << 20),
    )(*arrays)


def columns(tok_ref, start, width):
    return tok_ref.at[:, pl.ds(pl.multiple_of(start, 128), width)]


def started(copies):
    for copy in copies:
        copy.start()
    return copies


def cost(rows, width, cols):
    return pl.CostEstimate(
        flops=2 * rows * width * cols, bytes_accessed=2 * rows * width, transcendentals=0
    )


def grad_kernel(names, n_recv, tok_ref, grad_ref, *refs):
    groups = len(names) // 2
    recv, outs = refs[:n_recv], refs[n_recv : n_recv + groups]
    held, g_ref, sems = refs[n_recv + groups :]
    g_copy = pltpu.make_async_copy(grad_ref, g_ref, sems.at[len(names)])
    g_copy.start()
    copies = started(
        [
            pltpu.make_async_copy(
                columns(tok_ref, plane(core_index(), *name) * 512, 512),
                held.at[:, 512 * number : 512 * number + 512],
                sems.at[number],
            )
            for number, name in enumerate(names)
        ]
    )
    g_copy.wait()
    for number in range(len(names)):
        copies[number].wait()
        group, rows = number // 2, slice(512 * (number % 2), 512 * (number % 2) + 512)
        term = lax.dot_general(
            held[:, 512 * number : 512 * number + 512],
            g_ref[...],
            (((0,), (0,)), ((), ())),
            preferred_element_type=F32,
        )
        if recv:
            term = term + recv[group][rows].astype(F32)
        outs[group][rows] = term.astype(outs[group].dtype)


def grad_blocks(groups, dtype, limit, tokens, out_grad, *recv):
    names = [(k1, k2) for k1, half in groups for k2 in half]
    width, cols = 512 * len(names), out_grad.shape[1]
    return pl.pallas_call(
        functools.partial(grad_kernel, names, len(recv)),
        in_specs=[ANY, ANY] + [VMEM] * len(recv),
        out_specs=[VMEM] * len(groups),
        out_shape=[jax.ShapeDtypeStruct((1024, cols), dtype)] * len(groups),
        scratch_shapes=[
            pltpu.VMEM((tokens.shape[0], width), BF16),
            pltpu.VMEM(out_grad.shape, BF16),
            pltpu.SemaphoreType.DMA((len(names) + 1,)),
        ],
        compiler_params=pltpu.CompilerParams(vmem_limit_bytes=limit << 20),
        cost_estimate=cost(tokens.shape[0], width, cols),
    )(tokens, out_grad, *recv)


def total_kernel(own1, own2, got1, got2, *outs):
    mine = z_hi()
    for number, (own, got, start) in enumerate(
        ((own1, got1, 0), (own1, got1, 512), (own2, got2, 0), (own2, got2, 512))
    ):
        for which, out in ((1 - mine, outs[number]), (mine, outs[4 + number])):
            rows = pl.ds(pl.multiple_of(start + which * 256, 256), 256)
            out[...] = (own[rows] + got[rows].astype(F32)).astype(out.dtype)


def sum_kernel(zero, *refs):
    *refs, out = refs
    total = zero[...]
    for ref in refs:
        total = total + ref[...].astype(F32)
    out[...] = total.astype(out.dtype)


def reduce_scatter(tokens, out_grad):
    def send(arrays):
        return permute(arrays[0], first(1)), permute(arrays[1], first(-1))

    def blocks(groups, dtype, limit, *recv):
        return grad_blocks(groups, dtype, limit, tokens, out_grad, *recv)

    up1, down1 = send(blocks([(2, H1), (2, H2)], BF16, 50))
    up2, down2 = send(blocks([(1, H2), (3, H1)], BF16, 46))
    up3, down3 = send(blocks([(1, H1), (3, H2)], BF16, 46, up1, down1))
    own1, own2 = blocks([(0, H1), (0, H2)], F32, 46, down2, up2)
    block = (256, 512)
    sums = local(
        total_kernel,
        [(block, BF16), (block, BF16), (block, BF16), (block, F32)] * 2,
        own1,
        own2,
        up3,
        down3,
    )

    def exchange(two, one, three, zero):
        return zero, permute(two, second(2)), permute(one, second(1)), permute(three, second(-1))

    (give,) = local(sum_kernel, [(block, BF16)], *exchange(*sums[:4]))
    (keep,) = local(sum_kernel, [(block, F32)], *exchange(*sums[4:]))
    give, tokens = lax.optimization_barrier((give, tokens))
    got, held = lax.optimization_barrier((permute(give, across), arrange(ORDER, tokens)))
    return keep, got, held


def update_kernel(
    scale, keep, got, inner_ref, first_ref, second_ref, first_out, second_out, mine, other
):
    grad = (keep[...] + got[...].astype(F32)) * scale
    new_first = 0.9 * first_ref[...] + 0.1 * grad
    new_second = 0.95 * second_ref[...] + 0.05 * grad * grad
    inner = inner_ref[...]
    stepped = inner - 0.25 * (new_first / (jnp.sqrt(new_second) + 1e-08) + 0.1 * inner)
    first_out[...] = new_first
    second_out[...] = new_second
    half = stepped.shape[1] // 2
    core = core_index()
    for which, out in ((core, mine), (1 - core, other)):
        out[...] = jnp.where(which == 0, stepped[:, :half], stepped[:, half:])


def add_kernel(left, right, out):
    out[...] = (left[...].astype(F32) + right[...].astype(F32)).astype(out.dtype)


def outer(total, weights, momentum, n_replica):
    pseudo = weights - total / n_replica
    new_momentum = 0.9 * momentum + pseudo
    return weights - 0.7 * (pseudo + 0.9 * new_momentum), new_momentum


def synced_kernel(n_replica, left, right, weights_ref, momentum_ref, total, synced):
    half = left.shape[1]
    both = left[...].astype(F32) + right[...].astype(F32)
    total[...] = both
    low = core_index() == 0
    weights, momentum = (
        jnp.where(low, ref[:, :half], ref[:, half:]) for ref in (weights_ref, momentum_ref)
    )
    synced[...] = outer(both, weights, momentum, n_replica)[0].astype(BF16)


def outer_kernel(n_replica, mine, theirs, weights_ref, momentum_ref, weights_out, momentum_out):
    half = mine.shape[1]
    low = core_index() == 0
    left, right = mine[...], theirs[...]
    for part, total in (
        (slice(0, half), jnp.where(low, left, right)),
        (slice(half, 2 * half), jnp.where(low, right, left)),
    ):
        weights_out[:, part], momentum_out[:, part] = outer(
            total, weights_ref[:, part], momentum_ref[:, part], n_replica
        )


def join_kernel(mine, one, two, out):
    half = mine.shape[1]
    core = core_index()
    own = z_hi() == core
    same = jnp.where(own, mine[...], one[...])
    cross = jnp.where(own, one[...], two[...])
    out[:, :half] = jnp.where(core == 0, same, cross)
    out[:, half:] = jnp.where(core == 0, cross, same)


def mid_kernel(*refs):
    *ins, mid, near = refs
    for number, ref in enumerate(ins):
        near[256 * number : 256 * number + 256] = ref[...]
        if number < 3:
            mid[256 * number : 256 * number + 256] = ref[...]


def cut_kernel(up, down, up_out, down_out):
    rows = up_out.shape[0]
    up_out[...] = up[:rows]
    down_out[...] = down[rows:]


def arrange_kernel(places, tok_ref, out, sems):
    core = core_index()
    copies = started(
        [
            pltpu.make_async_copy(
                columns(tok_ref, plane(who, *place) * 512 + who * 256, 256),
                out.at[:, 256 * number : 256 * number + 256],
                sems.at[number],
            )
            for number, (partner, place) in enumerate(places)
            for who in (1 - core if partner else core,)
        ]
    )
    for copy in copies:
        copy.wait()


def arrange(places, tokens):
    return pl.pallas_call(
        functools.partial(arrange_kernel, places),
        in_specs=[ANY],
        out_specs=VMEM,
        out_shape=jax.ShapeDtypeStruct((tokens.shape[0], 256 * len(places)), BF16),
        scratch_shapes=[pltpu.SemaphoreType.DMA((len(places),))],
        compiler_params=pltpu.CompilerParams(vmem_limit_bytes=34 << 20),
        cost_estimate=SMALL,
    )(tokens)


def project_kernel(start, carried, scale, held, *refs):
    *arrays, out, right, sems = refs
    if carried:
        *arrays, acc = arrays
    copies, at = [], 0
    for number, ref in enumerate(arrays):
        rows = ref.shape[0]
        copies.append(pltpu.make_async_copy(ref, right.at[at : at + rows], sems.at[number]))
        at += rows
    for copy in started(copies):
        copy.wait()
    total = jnp.dot(held[:, start : start + at], right[...], preferred_element_type=F32)
    if carried:
        total = total + acc[...]
    out[...] = total if scale is None else (total * scale).astype(BF16)


def project(held, start, arrays, acc, scale):
    carried = [] if acc is None else [acc]
    rows, cols = held.shape[0], arrays[0].shape[1]
    return pl.pallas_call(
        functools.partial(project_kernel, start, bool(carried), scale),
        in_specs=[VMEM] * (1 + len(arrays) + len(carried)),
        out_specs=VMEM,
        out_shape=jax.ShapeDtypeStruct((rows, cols), F32 if scale is None else BF16),
        scratch_shapes=[
            pltpu.VMEM((sum(array.shape[0] for array in arrays), cols), BF16),
            pltpu.SemaphoreType.DMA((len(arrays),)),
        ],
        compiler_params=pltpu.CompilerParams(vmem_limit_bytes=16 << 20),
        cost_estimate=SMALL,
    )(held, *arrays, *carried)


def swap(arrays):
    return [permute(array, other_core) for array in arrays]


NEAR = [(3, 0), (1, 0), (2, 0), (0, 0), (0, 3), (0, 1)]
MIDDLE = [(3, 3), (1, 3), (2, 3), (3, 1), (1, 1), (2, 1)]
FAR = [(0, 2), (3, 2), (1, 2), (2, 2)]
ORDER = [
    (partner, place) for part in (NEAR, MIDDLE, FAR) for partner in range(2) for place in part
]


def gather_project(synced, held, scale, finish):
    quarter = ((256, 512), BF16)
    (own,) = local(
        join_kernel, [quarter], synced, permute(synced, halves_one), permute(synced, halves_two)
    )
    own_down, own_up = permute(own, second(-1)), permute(own, second(1))
    far = permute(own, first(2))
    ahead, behind = permute(own, first(-1)), permute(own, first(1))
    behind, ahead, far, own_up, own_down = lax.optimization_barrier(
        (behind, ahead, far, own_up, own_down)
    )
    mid, one = local(
        mid_kernel,
        [((768, 512), BF16), ((1536, 512), BF16)],
        behind,
        ahead,
        far,
        own,
        own_up,
        own_down,
    )
    mid_up, mid_down = permute(mid, second(1)), permute(mid, second(-1))
    own_far = permute(own_up, second(1))
    acc = project(held, 0, [one, *swap([one])], None, None)
    mid_up, mid_down, acc = lax.optimization_barrier((mid_up, mid_down, acc))
    cut_up, cut_down = local(
        cut_kernel, [((256, 512), BF16), ((512, 512), BF16)], mid_up, mid_down
    )
    far_down, far_up = permute(cut_down, second(-1)), permute(cut_up, second(1))
    two = [mid_up, mid_down]
    theirs = swap(two)
    finished = finish(acc)
    acc = project(held, 3072, two, acc, None)
    acc = project(held, 4608, theirs, acc, None)
    three = [own_far, far_up, far_down]
    *three, acc, new_global, new_momentum = lax.optimization_barrier((*three, acc, *finished))
    theirs = swap(three)
    acc = project(held, 6144, three, acc, None)
    return project(held, 7168, theirs, acc, scale), new_global, new_momentum


def body(
    tokens, out_grad, inner_weights, first_moment, second_moment, global_weights, outer_momentum
):
    scale = 1.0 / tokens.shape[1] ** 0.5
    n_replica = lax.axis_size("replica")
    keep, got, held = reduce_scatter(tokens, out_grad)
    block, half = keep.shape, (keep.shape[0], keep.shape[1] // 2)
    new_first, new_second, mine, other = local(
        functools.partial(update_kernel, scale),
        [(block, F32), (block, F32), (half, F32), (half, F32)],
        keep,
        got,
        inner_weights[0],
        first_moment[0],
        second_moment[0],
    )
    (mine,) = local(add_kernel, [(half, BF16)], mine, permute(other, other_core))
    total, synced = local(
        functools.partial(synced_kernel, n_replica),
        [(half, F32), (half, BF16)],
        mine,
        permute(mine, pair_lo),
        global_weights,
        outer_momentum,
    )

    def finish(after):
        mine, _ = lax.optimization_barrier((total, after))
        return local(
            functools.partial(outer_kernel, n_replica),
            [(block, F32), (block, F32)],
            mine,
            permute(mine, other_core),
            global_weights,
            outer_momentum,
        )

    projected, new_global, new_momentum = gather_project(synced, held, scale, finish)
    return (new_first[None], new_second[None], new_global, new_momentum, projected)


def solution(mesh):
    placed = (
        P(("replica", "fsdp"), None),
        P(("replica", "fsdp"), None),
        P("replica", "fsdp", None),
        P("replica", "fsdp", None),
        P("replica", "fsdp", None),
        P("fsdp", None),
        P("fsdp", None),
    )
    return jax.shard_map(
        body,
        mesh=mesh,
        in_specs=placed,
        out_specs=(
            P("replica", "fsdp", None),
            P("replica", "fsdp", None),
            P("fsdp", None),
            P("fsdp", None),
            P(("replica", "fsdp"), None),
        ),
        check_vma=False,
    )
```

```python
import functools

import jax
import jax.numpy as jnp
from jax import lax
from jax.experimental import pallas as pl
from jax.experimental.pallas import tpu as pltpu
from jax.sharding import PartitionSpec as P

BOTH = ("replica", "fsdp")
BF16, F32 = jnp.bfloat16, jnp.float32
H1, H2 = (2, 1), (3, 0)
VMEM = pl.BlockSpec(memory_space=pltpu.VMEM)
ANY = pl.BlockSpec(memory_space=pl.ANY)
SMALL = pl.CostEstimate(flops=1, bytes_accessed=1, transcendentals=0)


def flat(x, y, z, c):
    x, y, z = x % 4, y % 4, z % 4
    return ((z % 2) * 2 + c) * 32 + (y * 4 + x) * 2 + z // 2


def permute(array, move):
    pairs = []
    for x in range(4):
        for y in range(4):
            for z in range(4):
                for c in range(2):
                    target = move(x, y, z, c)
                    if target is not None:
                        pairs.append((flat(x, y, z, c), flat(*target)))
    return lax.ppermute(array, BOTH, pairs)


def first(step):
    return lambda x, y, z, c: (x, y + step, z, c) if c else (x + step, y, z, c)


def second(step):
    return lambda x, y, z, c: (x + step, y, z, c) if c else (x, y + step, z, c)


def other_core(x, y, z, c):
    return x, y, z, 1 - c


def pair_lo(x, y, z, c):
    return x, y, z ^ 1, c


def halves_one(x, y, z, c):
    return (x, y, 3 - z, c) if z // 2 == c else (x, y, z, 1 - c)


def halves_two(x, y, z, c):
    return None if z // 2 == c else (x, y, 3 - z, 1 - c)


def across(x, y, z, c):
    return x, y, z + 2, c


def z_hi():
    return lax.rem(lax.axis_index("fsdp"), 2)


def core_index():
    return lax.rem(lax.axis_index("replica"), 2)


def plane(core, k1, k2):
    f = lax.axis_index("fsdp")
    y, x = lax.div(f, 8), lax.rem(lax.div(f, 2), 4)
    dx, dy = k1 + core * (k2 - k1), k2 + core * (k1 - k2)
    return lax.rem(y + dy, 4) * 4 + lax.rem(x + dx, 4)


def local(kernel, outs, *arrays, limit=16):
    return pl.pallas_call(
        kernel,
        in_specs=[VMEM] * len(arrays),
        out_specs=[VMEM] * len(outs),
        out_shape=[jax.ShapeDtypeStruct(*out) for out in outs],
        compiler_params=pltpu.CompilerParams(vmem_limit_bytes=limit << 20),
    )(*arrays)


def columns(tok_ref, start, width):
    return tok_ref.at[:, pl.ds(pl.multiple_of(start, 128), width)]


def started(copies):
    for copy in copies:
        copy.start()
    return copies


def cost(rows, width, cols):
    return pl.CostEstimate(
        flops=2 * rows * width * cols, bytes_accessed=2 * rows * width, transcendentals=0
    )


def grad_kernel(names, n_recv, tok_ref, grad_ref, *refs):
    groups = len(names) // 2
    recv, outs = refs[:n_recv], refs[n_recv : n_recv + groups]
    held, g_ref, sems = refs[n_recv + groups :]
    g_copy = pltpu.make_async_copy(grad_ref, g_ref, sems.at[len(names)])
    g_copy.start()
    copies = started(
        [
            pltpu.make_async_copy(
                columns(tok_ref, plane(core_index(), *name) * 512, 512),
                held.at[:, 512 * number : 512 * number + 512],
                sems.at[number],
            )
            for number, name in enumerate(names)
        ]
    )
    g_copy.wait()
    for number in range(len(names)):
        copies[number].wait()
        group, rows = number // 2, slice(512 * (number % 2), 512 * (number % 2) + 512)
        term = lax.dot_general(
            held[:, 512 * number : 512 * number + 512],
            g_ref[...],
            (((0,), (0,)), ((), ())),
            preferred_element_type=F32,
        )
        if recv:
            term = term + recv[group][rows].astype(F32)
        outs[group][rows] = term.astype(outs[group].dtype)


def grad_blocks(groups, dtype, limit, tokens, out_grad, *recv):
    names = [(k1, k2) for k1, half in groups for k2 in half]
    width, cols = 512 * len(names), out_grad.shape[1]
    return pl.pallas_call(
        functools.partial(grad_kernel, names, len(recv)),
        in_specs=[ANY, ANY] + [VMEM] * len(recv),
        out_specs=[VMEM] * len(groups),
        out_shape=[jax.ShapeDtypeStruct((1024, cols), dtype)] * len(groups),
        scratch_shapes=[
            pltpu.VMEM((tokens.shape[0], width), BF16),
            pltpu.VMEM(out_grad.shape, BF16),
            pltpu.SemaphoreType.DMA((len(names) + 1,)),
        ],
        compiler_params=pltpu.CompilerParams(vmem_limit_bytes=limit << 20),
        cost_estimate=cost(tokens.shape[0], width, cols),
    )(tokens, out_grad, *recv)


def total_kernel(own1, own2, got1, got2, *outs):
    mine = z_hi()
    for number, (own, got, start) in enumerate(
        ((own1, got1, 0), (own1, got1, 512), (own2, got2, 0), (own2, got2, 512))
    ):
        for which, out in ((1 - mine, outs[number]), (mine, outs[4 + number])):
            rows = pl.ds(pl.multiple_of(start + which * 256, 256), 256)
            out[...] = (own[rows] + got[rows].astype(F32)).astype(out.dtype)


def sum_kernel(zero, *refs):
    *refs, out = refs
    total = zero[...]
    for ref in refs:
        total = total + ref[...].astype(F32)
    out[...] = total.astype(out.dtype)


def reduce_scatter(tokens, out_grad):
    def send(arrays):
        return permute(arrays[0], first(1)), permute(arrays[1], first(-1))

    def blocks(groups, dtype, limit, *recv):
        return grad_blocks(groups, dtype, limit, tokens, out_grad, *recv)

    up1, down1 = send(blocks([(2, H1), (2, H2)], BF16, 50))
    up2, down2 = send(blocks([(1, H2), (3, H1)], BF16, 46))
    up3, down3 = send(blocks([(1, H1), (3, H2)], BF16, 46, up1, down1))
    own1, own2 = blocks([(0, H1), (0, H2)], F32, 46, down2, up2)
    block = (256, 512)
    sums = local(
        total_kernel,
        [(block, BF16), (block, BF16), (block, BF16), (block, F32)] * 2,
        own1,
        own2,
        up3,
        down3,
    )

    def exchange(two, one, three, zero):
        return zero, permute(two, second(2)), permute(one, second(1)), permute(three, second(-1))

    (give,) = local(sum_kernel, [(block, BF16)], *exchange(*sums[:4]))
    (keep,) = local(sum_kernel, [(block, F32)], *exchange(*sums[4:]))
    give, tokens = lax.optimization_barrier((give, tokens))
    got, held = lax.optimization_barrier((permute(give, across), arrange(ORDER, tokens)))
    return keep, got, held


def update_kernel(
    scale, keep, got, inner_ref, first_ref, second_ref, first_out, second_out, mine, other
):
    grad = (keep[...] + got[...].astype(F32)) * scale
    new_first = 0.9 * first_ref[...] + 0.1 * grad
    new_second = 0.95 * second_ref[...] + 0.05 * grad * grad
    inner = inner_ref[...]
    stepped = inner - 0.25 * (new_first / (jnp.sqrt(new_second) + 1e-08) + 0.1 * inner)
    first_out[...] = new_first
    second_out[...] = new_second
    half = stepped.shape[1] // 2
    core = core_index()
    for which, out in ((core, mine), (1 - core, other)):
        out[...] = jnp.where(which == 0, stepped[:, :half], stepped[:, half:])


def add_kernel(left, right, out):
    out[...] = (left[...].astype(F32) + right[...].astype(F32)).astype(out.dtype)


def outer(total, weights, momentum, n_replica):
    pseudo = weights - total / n_replica
    new_momentum = 0.9 * momentum + pseudo
    return weights - 0.7 * (pseudo + 0.9 * new_momentum), new_momentum


def synced_kernel(n_replica, left, right, weights_ref, momentum_ref, total, synced):
    half = left.shape[1]
    both = left[...].astype(F32) + right[...].astype(F32)
    total[...] = both
    low = core_index() == 0
    weights, momentum = (
        jnp.where(low, ref[:, :half], ref[:, half:]) for ref in (weights_ref, momentum_ref)
    )
    synced[...] = outer(both, weights, momentum, n_replica)[0].astype(BF16)


def outer_kernel(n_replica, mine, theirs, weights_ref, momentum_ref, weights_out, momentum_out):
    half = mine.shape[1]
    low = core_index() == 0
    left, right = mine[...], theirs[...]
    for part, total in (
        (slice(0, half), jnp.where(low, left, right)),
        (slice(half, 2 * half), jnp.where(low, right, left)),
    ):
        weights_out[:, part], momentum_out[:, part] = outer(
            total, weights_ref[:, part], momentum_ref[:, part], n_replica
        )


def join_kernel(mine, one, two, out):
    half = mine.shape[1]
    core = core_index()
    own = z_hi() == core
    same = jnp.where(own, mine[...], one[...])
    cross = jnp.where(own, one[...], two[...])
    out[:, :half] = jnp.where(core == 0, same, cross)
    out[:, half:] = jnp.where(core == 0, cross, same)


def stack_kernel(*refs):
    ins, (low, high, near) = refs[:4], refs[4:]
    for number, ref in enumerate(ins):
        near[256 * number : 256 * number + 256] = ref[...]
        at = 256 * (number % 2)
        (low, high)[number // 2][at : at + 256] = ref[...]


def arrange_kernel(places, tok_ref, out, sems):
    core = core_index()
    copies = started(
        [
            pltpu.make_async_copy(
                columns(tok_ref, plane(who, *place) * 512 + who * 256, 256),
                out.at[:, 256 * number : 256 * number + 256],
                sems.at[number],
            )
            for number, (partner, place) in enumerate(places)
            for who in (1 - core if partner else core,)
        ]
    )
    for copy in copies:
        copy.wait()


def arrange(places, tokens):
    return pl.pallas_call(
        functools.partial(arrange_kernel, places),
        in_specs=[ANY],
        out_specs=VMEM,
        out_shape=jax.ShapeDtypeStruct((tokens.shape[0], 256 * len(places)), BF16),
        scratch_shapes=[pltpu.SemaphoreType.DMA((len(places),))],
        compiler_params=pltpu.CompilerParams(vmem_limit_bytes=34 << 20),
        cost_estimate=SMALL,
    )(tokens)


def project_kernel(start, carried, scale, held, *refs):
    *arrays, out, right, sems = refs
    if carried:
        *arrays, acc = arrays
    copies, at = [], 0
    for number, ref in enumerate(arrays):
        rows = ref.shape[0]
        copies.append(pltpu.make_async_copy(ref, right.at[at : at + rows], sems.at[number]))
        at += rows
    for copy in started(copies):
        copy.wait()
    total = jnp.dot(held[:, start : start + at], right[...], preferred_element_type=F32)
    if carried:
        total = total + acc[...]
    out[...] = total if scale is None else (total * scale).astype(BF16)


def project(held, start, arrays, acc, scale):
    carried = [] if acc is None else [acc]
    rows, cols = held.shape[0], arrays[0].shape[1]
    return pl.pallas_call(
        functools.partial(project_kernel, start, bool(carried), scale),
        in_specs=[VMEM] * (1 + len(arrays) + len(carried)),
        out_specs=VMEM,
        out_shape=jax.ShapeDtypeStruct((rows, cols), F32 if scale is None else BF16),
        scratch_shapes=[
            pltpu.VMEM((sum(array.shape[0] for array in arrays), cols), BF16),
            pltpu.SemaphoreType.DMA((len(arrays),)),
        ],
        compiler_params=pltpu.CompilerParams(vmem_limit_bytes=16 << 20),
        cost_estimate=SMALL,
    )(held, *arrays, *carried)


def join_pair_kernel(left, right, out):
    rows = left.shape[0]
    out[:rows] = left[...]
    out[rows:] = right[...]


def join(left, right):
    (both,) = local(join_pair_kernel, [((1024, 512), BF16)], left, right)
    return both


ORDER = [
    (partner, place)
    for part in (
        [(0, 0), (3, 0), (1, 0), (2, 0)],
        [(0, 3), (3, 3), (1, 1), (2, 1)],
        [(1, 3), (2, 3), (0, 1), (3, 1)],
        [(0, 2), (3, 2), (1, 2), (2, 2)],
    )
    for partner in range(2)
    for place in part
]


def gather_project(synced, held, scale, finish):
    quarter = ((256, 512), BF16)
    (own,) = local(
        join_kernel, [quarter], synced, permute(synced, halves_one), permute(synced, halves_two)
    )
    far = permute(own, first(2))
    ahead, behind = permute(own, first(-1)), permute(own, first(1))
    half = ((512, 512), BF16)
    low, high, near = local(
        stack_kernel, [half, half, ((1024, 512), BF16)], own, behind, ahead, far
    )
    low_up, high_down = permute(low, second(1)), permute(high, second(-1))
    high_up, low_down = permute(high, second(1)), permute(low, second(-1))
    acc = project(held, 0, [near, permute(near, other_core)], None, None)
    low_up, high_down, acc = lax.optimization_barrier((low_up, high_down, acc))
    far_low, far_high = permute(low_up, second(1)), permute(high_down, second(-1))
    wave = join(low_up, high_down)
    acc = project(held, 2048, [wave, permute(wave, other_core)], acc, None)
    finished = finish(acc)
    wave = join(high_up, low_down)
    acc = project(held, 4096, [wave, permute(wave, other_core)], acc, None)
    far_low, far_high, acc, new_global, new_momentum = lax.optimization_barrier(
        (far_low, far_high, acc, *finished)
    )
    wave = join(far_low, far_high)
    theirs = permute(wave, other_core)
    acc = project(held, 6144, [wave], acc, None)
    return project(held, 7168, [theirs], acc, scale), new_global, new_momentum


def body(
    tokens, out_grad, inner_weights, first_moment, second_moment, global_weights, outer_momentum
):
    scale = 1.0 / tokens.shape[1] ** 0.5
    n_replica = lax.axis_size("replica")
    keep, got, held = reduce_scatter(tokens, out_grad)
    block, half = keep.shape, (keep.shape[0], keep.shape[1] // 2)
    new_first, new_second, mine, other = local(
        functools.partial(update_kernel, scale),
        [(block, F32), (block, F32), (half, F32), (half, F32)],
        keep,
        got,
        inner_weights[0],
        first_moment[0],
        second_moment[0],
    )
    (mine,) = local(add_kernel, [(half, BF16)], mine, permute(other, other_core))
    total, synced = local(
        functools.partial(synced_kernel, n_replica),
        [(half, F32), (half, BF16)],
        mine,
        permute(mine, pair_lo),
        global_weights,
        outer_momentum,
    )

    def finish(after):
        mine, _ = lax.optimization_barrier((total, after))
        return local(
            functools.partial(outer_kernel, n_replica),
            [(block, F32), (block, F32)],
            mine,
            permute(mine, other_core),
            global_weights,
            outer_momentum,
        )

    projected, new_global, new_momentum = gather_project(synced, held, scale, finish)
    return (new_first[None], new_second[None], new_global, new_momentum, projected)


def solution(mesh):
    placed = (
        P(("replica", "fsdp"), None),
        P(("replica", "fsdp"), None),
        P("replica", "fsdp", None),
        P("replica", "fsdp", None),
        P("replica", "fsdp", None),
        P("fsdp", None),
        P("fsdp", None),
    )
    return jax.shard_map(
        body,
        mesh=mesh,
        in_specs=placed,
        out_specs=(
            P("replica", "fsdp", None),
            P("replica", "fsdp", None),
            P("fsdp", None),
            P("fsdp", None),
            P(("replica", "fsdp"), None),
        ),
        check_vma=False,
    )
```

```python
import functools

import jax
import jax.numpy as jnp
from jax import lax
from jax.experimental import pallas as pl
from jax.experimental.pallas import tpu as pltpu
from jax.sharding import PartitionSpec as P

BOTH = ("replica", "fsdp")
BF16, F32 = jnp.bfloat16, jnp.float32
H1, H2 = (2, 1), (3, 0)
VMEM = pl.BlockSpec(memory_space=pltpu.VMEM)
ANY = pl.BlockSpec(memory_space=pl.ANY)
SMALL = pl.CostEstimate(flops=1, bytes_accessed=1, transcendentals=0)


def flat(x, y, z, c):
    x, y, z = x % 4, y % 4, z % 4
    return ((z % 2) * 2 + c) * 32 + (y * 4 + x) * 2 + z // 2


def permute(array, move):
    pairs = []
    for x in range(4):
        for y in range(4):
            for z in range(4):
                for c in range(2):
                    target = move(x, y, z, c)
                    if target is not None:
                        pairs.append((flat(x, y, z, c), flat(*target)))
    return lax.ppermute(array, BOTH, pairs)


def first(step):
    return lambda x, y, z, c: (x, y + step, z, c) if c else (x + step, y, z, c)


def second(step):
    return lambda x, y, z, c: (x + step, y, z, c) if c else (x, y + step, z, c)


def other_core(x, y, z, c):
    return x, y, z, 1 - c


def pair_lo(x, y, z, c):
    return x, y, z ^ 1, c


def halves_one(x, y, z, c):
    return (x, y, 3 - z, c) if z // 2 == c else (x, y, z, 1 - c)


def halves_two(x, y, z, c):
    return None if z // 2 == c else (x, y, 3 - z, 1 - c)


def across(x, y, z, c):
    return x, y, z + 2, c


def z_hi():
    return lax.rem(lax.axis_index("fsdp"), 2)


def core_index():
    return lax.rem(lax.axis_index("replica"), 2)


def plane(core, k1, k2):
    f = lax.axis_index("fsdp")
    y, x = lax.div(f, 8), lax.rem(lax.div(f, 2), 4)
    dx, dy = k1 + core * (k2 - k1), k2 + core * (k1 - k2)
    return lax.rem(y + dy, 4) * 4 + lax.rem(x + dx, 4)


def local(kernel, outs, *arrays, limit=16):
    return pl.pallas_call(
        kernel,
        in_specs=[VMEM] * len(arrays),
        out_specs=[VMEM] * len(outs),
        out_shape=[jax.ShapeDtypeStruct(*out) for out in outs],
        compiler_params=pltpu.CompilerParams(vmem_limit_bytes=limit << 20),
    )(*arrays)


def columns(tok_ref, start, width):
    return tok_ref.at[:, pl.ds(pl.multiple_of(start, 128), width)]


def started(copies):
    for copy in copies:
        copy.start()
    return copies


def cost(rows, width, cols):
    return pl.CostEstimate(
        flops=2 * rows * width * cols, bytes_accessed=2 * rows * width, transcendentals=0
    )


def grad_kernel(names, n_recv, tok_ref, grad_ref, *refs):
    groups = len(names) // 2
    recv, outs = refs[:n_recv], refs[n_recv : n_recv + groups]
    held, g_ref, sems = refs[n_recv + groups :]
    g_copy = pltpu.make_async_copy(grad_ref, g_ref, sems.at[len(names)])
    g_copy.start()
    copies = started(
        [
            pltpu.make_async_copy(
                columns(tok_ref, plane(core_index(), *name) * 512, 512),
                held.at[:, 512 * number : 512 * number + 512],
                sems.at[number],
            )
            for number, name in enumerate(names)
        ]
    )
    g_copy.wait()
    for number in range(len(names)):
        copies[number].wait()
        group, rows = number // 2, slice(512 * (number % 2), 512 * (number % 2) + 512)
        term = lax.dot_general(
            held[:, 512 * number : 512 * number + 512],
            g_ref[...],
            (((0,), (0,)), ((), ())),
            preferred_element_type=F32,
        )
        if recv:
            term = term + recv[group][rows].astype(F32)
        outs[group][rows] = term.astype(outs[group].dtype)


def grad_blocks(groups, dtype, limit, tokens, out_grad, *recv):
    names = [(k1, k2) for k1, half in groups for k2 in half]
    width, cols = 512 * len(names), out_grad.shape[1]
    return pl.pallas_call(
        functools.partial(grad_kernel, names, len(recv)),
        in_specs=[ANY, ANY] + [VMEM] * len(recv),
        out_specs=[VMEM] * len(groups),
        out_shape=[jax.ShapeDtypeStruct((1024, cols), dtype)] * len(groups),
        scratch_shapes=[
            pltpu.VMEM((tokens.shape[0], width), BF16),
            pltpu.VMEM(out_grad.shape, BF16),
            pltpu.SemaphoreType.DMA((len(names) + 1,)),
        ],
        compiler_params=pltpu.CompilerParams(vmem_limit_bytes=limit << 20),
        cost_estimate=cost(tokens.shape[0], width, cols),
    )(tokens, out_grad, *recv)


def total_kernel(own1, own2, got1, got2, *outs):
    mine = z_hi()
    for number, (own, got, start) in enumerate(
        ((own1, got1, 0), (own1, got1, 512), (own2, got2, 0), (own2, got2, 512))
    ):
        for which, out in ((1 - mine, outs[number]), (mine, outs[4 + number])):
            rows = pl.ds(pl.multiple_of(start + which * 256, 256), 256)
            out[...] = (own[rows] + got[rows].astype(F32)).astype(out.dtype)


def sum_kernel(zero, *refs):
    *refs, out = refs
    total = zero[...]
    for ref in refs:
        total = total + ref[...].astype(F32)
    out[...] = total.astype(out.dtype)


def reduce_scatter(tokens, out_grad):
    def send(arrays):
        return permute(arrays[0], first(1)), permute(arrays[1], first(-1))

    def blocks(groups, dtype, limit, *recv):
        return grad_blocks(groups, dtype, limit, tokens, out_grad, *recv)

    up1, down1 = send(blocks([(2, H1), (2, H2)], BF16, 50))
    up2, down2 = send(blocks([(1, H2), (3, H1)], BF16, 46))
    up3, down3 = send(blocks([(1, H1), (3, H2)], BF16, 46, up1, down1))
    own1, own2 = blocks([(0, H1), (0, H2)], F32, 46, down2, up2)
    block = (256, 512)
    sums = local(
        total_kernel,
        [(block, BF16), (block, BF16), (block, BF16), (block, F32)] * 2,
        own1,
        own2,
        up3,
        down3,
    )

    def exchange(two, one, three, zero):
        return zero, permute(two, second(2)), permute(one, second(1)), permute(three, second(-1))

    (give,) = local(sum_kernel, [(block, BF16)], *exchange(*sums[:4]))
    (keep,) = local(sum_kernel, [(block, F32)], *exchange(*sums[4:]))
    give, tokens = lax.optimization_barrier((give, tokens))
    got, held = lax.optimization_barrier((permute(give, across), arrange(ORDER, tokens)))
    return keep, got, held


def update_kernel(
    scale, keep, got, inner_ref, first_ref, second_ref, first_out, second_out, mine, other
):
    grad = (keep[...] + got[...].astype(F32)) * scale
    new_first = 0.9 * first_ref[...] + 0.1 * grad
    new_second = 0.95 * second_ref[...] + 0.05 * grad * grad
    inner = inner_ref[...]
    stepped = inner - 0.25 * (new_first / (jnp.sqrt(new_second) + 1e-08) + 0.1 * inner)
    first_out[...] = new_first
    second_out[...] = new_second
    half = stepped.shape[1] // 2
    core = core_index()
    for which, out in ((core, mine), (1 - core, other)):
        out[...] = jnp.where(which == 0, stepped[:, :half], stepped[:, half:])


def add_kernel(left, right, out):
    out[...] = (left[...].astype(F32) + right[...].astype(F32)).astype(out.dtype)


def outer(total, weights, momentum, n_replica):
    pseudo = weights - total / n_replica
    new_momentum = 0.9 * momentum + pseudo
    return weights - 0.7 * (pseudo + 0.9 * new_momentum), new_momentum


def synced_kernel(n_replica, left, right, weights_ref, momentum_ref, total, synced):
    half = left.shape[1]
    both = left[...].astype(F32) + right[...].astype(F32)
    total[...] = both
    low = core_index() == 0
    weights, momentum = (
        jnp.where(low, ref[:, :half], ref[:, half:]) for ref in (weights_ref, momentum_ref)
    )
    synced[...] = outer(both, weights, momentum, n_replica)[0].astype(BF16)


def outer_kernel(n_replica, mine, theirs, weights_ref, momentum_ref, weights_out, momentum_out):
    half = mine.shape[1]
    low = core_index() == 0
    left, right = mine[...], theirs[...]
    for part, total in (
        (slice(0, half), jnp.where(low, left, right)),
        (slice(half, 2 * half), jnp.where(low, right, left)),
    ):
        weights_out[:, part], momentum_out[:, part] = outer(
            total, weights_ref[:, part], momentum_ref[:, part], n_replica
        )


def join_kernel(mine, one, two, out):
    half = mine.shape[1]
    core = core_index()
    own = z_hi() == core
    same = jnp.where(own, mine[...], one[...])
    cross = jnp.where(own, one[...], two[...])
    out[:, :half] = jnp.where(core == 0, same, cross)
    out[:, half:] = jnp.where(core == 0, cross, same)


def stack_kernel(*refs):
    ins, (low, high, near) = refs[:4], refs[4:]
    for number, ref in enumerate(ins):
        near[256 * number : 256 * number + 256] = ref[...]
        at = 256 * (number % 2)
        (low, high)[number // 2][at : at + 256] = ref[...]


def arrange_kernel(places, tok_ref, out, sems):
    core = core_index()
    copies = started(
        [
            pltpu.make_async_copy(
                columns(tok_ref, plane(who, *place) * 512 + who * 256, 256),
                out.at[:, 256 * number : 256 * number + 256],
                sems.at[number],
            )
            for number, (partner, place) in enumerate(places)
            for who in (1 - core if partner else core,)
        ]
    )
    for copy in copies:
        copy.wait()


def arrange(places, tokens):
    return pl.pallas_call(
        functools.partial(arrange_kernel, places),
        in_specs=[ANY],
        out_specs=VMEM,
        out_shape=jax.ShapeDtypeStruct((tokens.shape[0], 256 * len(places)), BF16),
        scratch_shapes=[pltpu.SemaphoreType.DMA((len(places),))],
        compiler_params=pltpu.CompilerParams(vmem_limit_bytes=34 << 20),
        cost_estimate=SMALL,
    )(tokens)


def project_kernel(start, carried, scale, held, *refs):
    *arrays, out, right, sems = refs
    if carried:
        *arrays, acc = arrays
    copies, at = [], 0
    for number, ref in enumerate(arrays):
        rows = ref.shape[0]
        copies.append(pltpu.make_async_copy(ref, right.at[at : at + rows], sems.at[number]))
        at += rows
    for copy in started(copies):
        copy.wait()
    total = jnp.dot(held[:, start : start + at], right[...], preferred_element_type=F32)
    if carried:
        total = total + acc[...]
    out[...] = total if scale is None else (total * scale).astype(BF16)


def project(held, start, arrays, acc, scale):
    carried = [] if acc is None else [acc]
    rows, cols = held.shape[0], arrays[0].shape[1]
    return pl.pallas_call(
        functools.partial(project_kernel, start, bool(carried), scale),
        in_specs=[VMEM] * (1 + len(arrays) + len(carried)),
        out_specs=VMEM,
        out_shape=jax.ShapeDtypeStruct((rows, cols), F32 if scale is None else BF16),
        scratch_shapes=[
            pltpu.VMEM((sum(array.shape[0] for array in arrays), cols), BF16),
            pltpu.SemaphoreType.DMA((len(arrays),)),
        ],
        compiler_params=pltpu.CompilerParams(vmem_limit_bytes=16 << 20),
        cost_estimate=SMALL,
    )(held, *arrays, *carried)


def join_pair_kernel(left, right, out):
    rows = left.shape[0]
    out[:rows] = left[...]
    out[rows:] = right[...]


def join(left, right):
    (both,) = local(join_pair_kernel, [((1024, 512), BF16)], left, right)
    return both


ORDER = [
    (partner, place)
    for part in (
        [(0, 0), (3, 0), (1, 0), (2, 0)],
        [(0, 3), (3, 3), (1, 1), (2, 1)],
        [(1, 3), (2, 3), (0, 1), (3, 1)],
        [(0, 2), (3, 2), (1, 2), (2, 2)],
    )
    for partner in range(2)
    for place in part
]


def gather_project(synced, held, scale, finish):
    quarter = ((256, 512), BF16)
    (own,) = local(
        join_kernel, [quarter], synced, permute(synced, halves_one), permute(synced, halves_two)
    )
    far = permute(own, first(2))
    ahead, behind = permute(own, first(-1)), permute(own, first(1))
    half = ((512, 512), BF16)
    low, high, near = local(
        stack_kernel, [half, half, ((1024, 512), BF16)], own, behind, ahead, far
    )
    low_up, high_down = permute(low, second(1)), permute(high, second(-1))
    high_up, low_down = permute(high, second(1)), permute(low, second(-1))
    acc = project(held, 0, [near, permute(near, other_core)], None, None)
    finished = finish(acc)
    low_up, high_down, acc = lax.optimization_barrier((low_up, high_down, acc))
    far_low, far_high = permute(low_up, second(1)), permute(high_down, second(-1))
    wave_one = join(low_up, high_down)
    acc = project(held, 2048, [wave_one], acc, None)
    wave_two = join(high_up, low_down)
    acc = project(held, 4096, [wave_two], acc, None)
    far_low, far_high, acc, new_global, new_momentum = lax.optimization_barrier(
        (far_low, far_high, acc, *finished)
    )
    wave = join(far_low, far_high)
    waves = [permute(array, other_core) for array in (wave_one, wave_two)]
    theirs = permute(wave, other_core)
    acc = project(held, 6144, [wave], acc, None)
    acc = project(held, 3072, waves[:1], acc, None)
    acc = project(held, 5120, waves[1:], acc, None)
    return project(held, 7168, [theirs], acc, scale), new_global, new_momentum


def body(
    tokens, out_grad, inner_weights, first_moment, second_moment, global_weights, outer_momentum
):
    scale = 1.0 / tokens.shape[1] ** 0.5
    n_replica = lax.axis_size("replica")
    keep, got, held = reduce_scatter(tokens, out_grad)
    block, half = keep.shape, (keep.shape[0], keep.shape[1] // 2)
    new_first, new_second, mine, other = local(
        functools.partial(update_kernel, scale),
        [(block, F32), (block, F32), (half, F32), (half, F32)],
        keep,
        got,
        inner_weights[0],
        first_moment[0],
        second_moment[0],
    )
    (mine,) = local(add_kernel, [(half, BF16)], mine, permute(other, other_core))
    total, synced = local(
        functools.partial(synced_kernel, n_replica),
        [(half, F32), (half, BF16)],
        mine,
        permute(mine, pair_lo),
        global_weights,
        outer_momentum,
    )

    def finish(after):
        mine, _ = lax.optimization_barrier((total, after))
        return local(
            functools.partial(outer_kernel, n_replica),
            [(block, F32), (block, F32)],
            mine,
            permute(mine, other_core),
            global_weights,
            outer_momentum,
        )

    projected, new_global, new_momentum = gather_project(synced, held, scale, finish)
    return (new_first[None], new_second[None], new_global, new_momentum, projected)


def solution(mesh):
    placed = (
        P(("replica", "fsdp"), None),
        P(("replica", "fsdp"), None),
        P("replica", "fsdp", None),
        P("replica", "fsdp", None),
        P("replica", "fsdp", None),
        P("fsdp", None),
        P("fsdp", None),
    )
    return jax.shard_map(
        body,
        mesh=mesh,
        in_specs=placed,
        out_specs=(
            P("replica", "fsdp", None),
            P("replica", "fsdp", None),
            P("fsdp", None),
            P("fsdp", None),
            P(("replica", "fsdp"), None),
        ),
        check_vma=False,
    )
```

```python
import functools

import jax
import jax.numpy as jnp
from jax import lax
from jax.experimental import pallas as pl
from jax.experimental.pallas import tpu as pltpu
from jax.sharding import PartitionSpec as P

BOTH = ("replica", "fsdp")
BF16, F32 = jnp.bfloat16, jnp.float32
H1, H2 = (2, 1), (3, 0)
VMEM = pl.BlockSpec(memory_space=pltpu.VMEM)
ANY = pl.BlockSpec(memory_space=pl.ANY)
SMALL = pl.CostEstimate(flops=1, bytes_accessed=1, transcendentals=0)


def flat(x, y, z, c):
    x, y, z = x % 4, y % 4, z % 4
    return ((z % 2) * 2 + c) * 32 + (y * 4 + x) * 2 + z // 2


def permute(array, move):
    pairs = []
    for x in range(4):
        for y in range(4):
            for z in range(4):
                for c in range(2):
                    target = move(x, y, z, c)
                    if target is not None:
                        pairs.append((flat(x, y, z, c), flat(*target)))
    return lax.ppermute(array, BOTH, pairs)


def first(step):
    return lambda x, y, z, c: (x, y + step, z, c) if c else (x + step, y, z, c)


def second(step):
    return lambda x, y, z, c: (x + step, y, z, c) if c else (x, y + step, z, c)


def other_core(x, y, z, c):
    return x, y, z, 1 - c


def pair_lo(x, y, z, c):
    return x, y, z ^ 1, c


def halves_one(x, y, z, c):
    return (x, y, 3 - z, c) if z // 2 == c else (x, y, z, 1 - c)


def halves_two(x, y, z, c):
    return None if z // 2 == c else (x, y, 3 - z, 1 - c)


def across(x, y, z, c):
    return x, y, z + 2, c


def z_hi():
    return lax.rem(lax.axis_index("fsdp"), 2)


def core_index():
    return lax.rem(lax.axis_index("replica"), 2)


def plane(core, k1, k2):
    f = lax.axis_index("fsdp")
    y, x = lax.div(f, 8), lax.rem(lax.div(f, 2), 4)
    dx, dy = k1 + core * (k2 - k1), k2 + core * (k1 - k2)
    return lax.rem(y + dy, 4) * 4 + lax.rem(x + dx, 4)


def local(kernel, outs, *arrays, limit=16):
    return pl.pallas_call(
        kernel,
        in_specs=[VMEM] * len(arrays),
        out_specs=[VMEM] * len(outs),
        out_shape=[jax.ShapeDtypeStruct(*out) for out in outs],
        compiler_params=pltpu.CompilerParams(vmem_limit_bytes=limit << 20),
    )(*arrays)


def columns(tok_ref, start, width):
    return tok_ref.at[:, pl.ds(pl.multiple_of(start, 128), width)]


def started(copies):
    for copy in copies:
        copy.start()
    return copies


def cost(rows, width, cols):
    return pl.CostEstimate(
        flops=2 * rows * width * cols, bytes_accessed=2 * rows * width, transcendentals=0
    )


def grad_kernel(names, n_recv, tok_ref, grad_ref, *refs):
    groups = len(names) // 2
    recv, outs = refs[:n_recv], refs[n_recv : n_recv + groups]
    held, g_ref, sems = refs[n_recv + groups :]
    g_copy = pltpu.make_async_copy(grad_ref, g_ref, sems.at[len(names)])
    g_copy.start()
    copies = started(
        [
            pltpu.make_async_copy(
                columns(tok_ref, plane(core_index(), *name) * 512, 512),
                held.at[:, 512 * number : 512 * number + 512],
                sems.at[number],
            )
            for number, name in enumerate(names)
        ]
    )
    g_copy.wait()
    for number in range(len(names)):
        copies[number].wait()
        group, rows = number // 2, slice(512 * (number % 2), 512 * (number % 2) + 512)
        term = lax.dot_general(
            held[:, 512 * number : 512 * number + 512],
            g_ref[...],
            (((0,), (0,)), ((), ())),
            preferred_element_type=F32,
        )
        if recv:
            term = term + recv[group][rows].astype(F32)
        outs[group][rows] = term.astype(outs[group].dtype)


def grad_blocks(groups, dtype, limit, tokens, out_grad, *recv):
    names = [(k1, k2) for k1, half in groups for k2 in half]
    width, cols = 512 * len(names), out_grad.shape[1]
    return pl.pallas_call(
        functools.partial(grad_kernel, names, len(recv)),
        in_specs=[ANY, ANY] + [VMEM] * len(recv),
        out_specs=[VMEM] * len(groups),
        out_shape=[jax.ShapeDtypeStruct((1024, cols), dtype)] * len(groups),
        scratch_shapes=[
            pltpu.VMEM((tokens.shape[0], width), BF16),
            pltpu.VMEM(out_grad.shape, BF16),
            pltpu.SemaphoreType.DMA((len(names) + 1,)),
        ],
        compiler_params=pltpu.CompilerParams(vmem_limit_bytes=limit << 20),
        cost_estimate=cost(tokens.shape[0], width, cols),
    )(tokens, out_grad, *recv)


def total_kernel(own1, own2, got1, got2, *outs):
    mine = z_hi()
    for number, (own, got, start) in enumerate(
        ((own1, got1, 0), (own1, got1, 512), (own2, got2, 0), (own2, got2, 512))
    ):
        for which, out in ((1 - mine, outs[number]), (mine, outs[4 + number])):
            rows = pl.ds(pl.multiple_of(start + which * 256, 256), 256)
            out[...] = (own[rows] + got[rows].astype(F32)).astype(out.dtype)


def sum_kernel(zero, *refs):
    *refs, out = refs
    total = zero[...]
    for ref in refs:
        total = total + ref[...].astype(F32)
    out[...] = total.astype(out.dtype)


def reduce_scatter(tokens, out_grad):
    def send(arrays):
        return permute(arrays[0], first(1)), permute(arrays[1], first(-1))

    def blocks(groups, dtype, limit, *recv):
        return grad_blocks(groups, dtype, limit, tokens, out_grad, *recv)

    up1, down1 = send(blocks([(2, H1), (2, H2)], BF16, 50))
    up2, down2 = send(blocks([(1, H2), (3, H1)], BF16, 46))
    up3, down3 = send(blocks([(1, H1), (3, H2)], BF16, 46, up1, down1))
    own1, own2 = blocks([(0, H1), (0, H2)], F32, 46, down2, up2)
    block = (256, 512)
    sums = local(
        total_kernel,
        [(block, BF16), (block, BF16), (block, BF16), (block, F32)] * 2,
        own1,
        own2,
        up3,
        down3,
    )

    def exchange(two, one, three, zero):
        return zero, permute(two, second(2)), permute(one, second(1)), permute(three, second(-1))

    (give,) = local(sum_kernel, [(block, BF16)], *exchange(*sums[:4]))
    (keep,) = local(sum_kernel, [(block, F32)], *exchange(*sums[4:]))
    give, tokens = lax.optimization_barrier((give, tokens))
    got, held = lax.optimization_barrier((permute(give, across), arrange(ORDER, tokens)))
    return keep, got, held


def update_kernel(
    scale, keep, got, inner_ref, first_ref, second_ref, first_out, second_out, mine, other
):
    grad = (keep[...] + got[...].astype(F32)) * scale
    new_first = 0.9 * first_ref[...] + 0.1 * grad
    new_second = 0.95 * second_ref[...] + 0.05 * grad * grad
    inner = inner_ref[...]
    stepped = inner - 0.25 * (new_first / (jnp.sqrt(new_second) + 1e-08) + 0.1 * inner)
    first_out[...] = new_first
    second_out[...] = new_second
    half = stepped.shape[1] // 2
    core = core_index()
    for which, out in ((core, mine), (1 - core, other)):
        out[...] = jnp.where(which == 0, stepped[:, :half], stepped[:, half:])


def add_kernel(left, right, out):
    out[...] = (left[...].astype(F32) + right[...].astype(F32)).astype(out.dtype)


def outer(total, weights, momentum, n_replica):
    pseudo = weights - total / n_replica
    new_momentum = 0.9 * momentum + pseudo
    return weights - 0.7 * (pseudo + 0.9 * new_momentum), new_momentum


def synced_kernel(n_replica, left, right, weights_ref, momentum_ref, total, synced):
    half = left.shape[1]
    both = left[...].astype(F32) + right[...].astype(F32)
    total[...] = both
    low = core_index() == 0
    weights, momentum = (
        jnp.where(low, ref[:, :half], ref[:, half:]) for ref in (weights_ref, momentum_ref)
    )
    synced[...] = outer(both, weights, momentum, n_replica)[0].astype(BF16)


def outer_kernel(n_replica, mine, theirs, weights_ref, momentum_ref, weights_out, momentum_out):
    half = mine.shape[1]
    low = core_index() == 0
    left, right = mine[...], theirs[...]
    for part, total in (
        (slice(0, half), jnp.where(low, left, right)),
        (slice(half, 2 * half), jnp.where(low, right, left)),
    ):
        weights_out[:, part], momentum_out[:, part] = outer(
            total, weights_ref[:, part], momentum_ref[:, part], n_replica
        )


def join_kernel(mine, one, two, out):
    half = mine.shape[1]
    core = core_index()
    own = z_hi() == core
    same = jnp.where(own, mine[...], one[...])
    cross = jnp.where(own, one[...], two[...])
    out[:, :half] = jnp.where(core == 0, same, cross)
    out[:, half:] = jnp.where(core == 0, cross, same)


def stack_kernel(*refs):
    ins, (low, high, near) = refs[:4], refs[4:]
    for number, ref in enumerate(ins):
        near[256 * number : 256 * number + 256] = ref[...]
        at = 256 * (number % 2)
        (low, high)[number // 2][at : at + 256] = ref[...]


def arrange_kernel(places, tok_ref, out, sems):
    core = core_index()
    copies = started(
        [
            pltpu.make_async_copy(
                columns(tok_ref, plane(who, *place) * 512 + who * 256, 256),
                out.at[:, 256 * number : 256 * number + 256],
                sems.at[number],
            )
            for number, (partner, place) in enumerate(places)
            for who in (1 - core if partner else core,)
        ]
    )
    for copy in copies:
        copy.wait()


def arrange(places, tokens):
    return pl.pallas_call(
        functools.partial(arrange_kernel, places),
        in_specs=[ANY],
        out_specs=VMEM,
        out_shape=jax.ShapeDtypeStruct((tokens.shape[0], 256 * len(places)), BF16),
        scratch_shapes=[pltpu.SemaphoreType.DMA((len(places),))],
        compiler_params=pltpu.CompilerParams(vmem_limit_bytes=34 << 20),
        cost_estimate=SMALL,
    )(tokens)


def project_kernel(start, carried, scale, held, *refs):
    *arrays, out, right, sems = refs
    if carried:
        *arrays, acc = arrays
    copies, at = [], 0
    for number, ref in enumerate(arrays):
        rows = ref.shape[0]
        copies.append(pltpu.make_async_copy(ref, right.at[at : at + rows], sems.at[number]))
        at += rows
    for copy in started(copies):
        copy.wait()
    total = jnp.dot(held[:, start : start + at], right[...], preferred_element_type=F32)
    if carried:
        total = total + acc[...]
    out[...] = total if scale is None else (total * scale).astype(BF16)


def project(held, start, arrays, acc, scale):
    carried = [] if acc is None else [acc]
    rows, cols = held.shape[0], arrays[0].shape[1]
    return pl.pallas_call(
        functools.partial(project_kernel, start, bool(carried), scale),
        in_specs=[VMEM] * (1 + len(arrays) + len(carried)),
        out_specs=VMEM,
        out_shape=jax.ShapeDtypeStruct((rows, cols), F32 if scale is None else BF16),
        scratch_shapes=[
            pltpu.VMEM((sum(array.shape[0] for array in arrays), cols), BF16),
            pltpu.SemaphoreType.DMA((len(arrays),)),
        ],
        compiler_params=pltpu.CompilerParams(vmem_limit_bytes=16 << 20),
        cost_estimate=SMALL,
    )(held, *arrays, *carried)


def join_pair_kernel(left, right, out):
    rows = left.shape[0]
    out[:rows] = left[...]
    out[rows:] = right[...]


def join(left, right):
    (both,) = local(join_pair_kernel, [((1024, 512), BF16)], left, right)
    return both


NEAR = [(0, 0), (3, 0), (1, 0), (2, 0)]
WAVES = [(0, 3), (3, 3), (1, 1), (2, 1), (1, 3), (2, 3), (0, 1), (3, 1)]
FAR = [(0, 2), (3, 2), (1, 2), (2, 2)]
ORDER = [
    (partner, place)
    for partner, part in (
        (0, NEAR), (1, NEAR), (0, WAVES), (1, WAVES), (0, FAR), (1, FAR)
    )
    for place in part
]


def gather_project(synced, held, scale, finish):
    quarter = ((256, 512), BF16)
    (own,) = local(
        join_kernel, [quarter], synced, permute(synced, halves_one), permute(synced, halves_two)
    )
    far = permute(own, first(2))
    ahead, behind = permute(own, first(-1)), permute(own, first(1))
    half = ((512, 512), BF16)
    low, high, near = local(
        stack_kernel, [half, half, ((1024, 512), BF16)], own, behind, ahead, far
    )
    low_up, high_down = permute(low, second(1)), permute(high, second(-1))
    high_up, low_down = permute(high, second(1)), permute(low, second(-1))
    acc = project(held, 0, [near, permute(near, other_core)], None, None)
    finished = finish(acc)
    low_up, high_down, acc = lax.optimization_barrier((low_up, high_down, acc))
    far_low, far_high = permute(low_up, second(1)), permute(high_down, second(-1))
    wave_one = join(low_up, high_down)
    wave_two = join(high_up, low_down)
    acc = project(held, 2048, [wave_one, wave_two], acc, None)
    far_low, far_high, acc, new_global, new_momentum = lax.optimization_barrier(
        (far_low, far_high, acc, *finished)
    )
    wave = join(far_low, far_high)
    waves = [permute(array, other_core) for array in (wave_one, wave_two)]
    theirs = permute(wave, other_core)
    acc = project(held, 4096, [*waves, wave], acc, None)
    return project(held, 7168, [theirs], acc, scale), new_global, new_momentum


def body(
    tokens, out_grad, inner_weights, first_moment, second_moment, global_weights, outer_momentum
):
    scale = 1.0 / tokens.shape[1] ** 0.5
    n_replica = lax.axis_size("replica")
    keep, got, held = reduce_scatter(tokens, out_grad)
    block, half = keep.shape, (keep.shape[0], keep.shape[1] // 2)
    new_first, new_second, mine, other = local(
        functools.partial(update_kernel, scale),
        [(block, F32), (block, F32), (half, F32), (half, F32)],
        keep,
        got,
        inner_weights[0],
        first_moment[0],
        second_moment[0],
    )
    (mine,) = local(add_kernel, [(half, BF16)], mine, permute(other, other_core))
    total, synced = local(
        functools.partial(synced_kernel, n_replica),
        [(half, F32), (half, BF16)],
        mine,
        permute(mine, pair_lo),
        global_weights,
        outer_momentum,
    )

    def finish(after):
        mine, _ = lax.optimization_barrier((total, after))
        return local(
            functools.partial(outer_kernel, n_replica),
            [(block, F32), (block, F32)],
            mine,
            permute(mine, other_core),
            global_weights,
            outer_momentum,
        )

    projected, new_global, new_momentum = gather_project(synced, held, scale, finish)
    return (new_first[None], new_second[None], new_global, new_momentum, projected)


def solution(mesh):
    placed = (
        P(("replica", "fsdp"), None),
        P(("replica", "fsdp"), None),
        P("replica", "fsdp", None),
        P("replica", "fsdp", None),
        P("replica", "fsdp", None),
        P("fsdp", None),
        P("fsdp", None),
    )
    return jax.shard_map(
        body,
        mesh=mesh,
        in_specs=placed,
        out_specs=(
            P("replica", "fsdp", None),
            P("replica", "fsdp", None),
            P("fsdp", None),
            P("fsdp", None),
            P(("replica", "fsdp"), None),
        ),
        check_vma=False,
    )
```
